32 devices in a mesh: dp: 16 (over z, y, x), tp: 2 (over core).
Axes of the slice: x: 2, y: 2, z: 4, core: 2. Of those that a mesh axis runs over, the one named last changes fastest.
Arguments:
- prefix_hidden: bfloat16 [1024, 7168], P('dp', 'tp'), may hold values from -6 to 6
- down_kv: bfloat16 [7168, 576], P('tp'), may hold values from -0.0625 to 0.0625
- latent_gain: float32 [512], replicated, may hold values from 0.1 to 1.9
- step_hidden: bfloat16 [128, 3, 7168], P('dp', None, 'tp'), may hold values from -6 to 6
- query_nope: bfloat16 [128, 3, 2048], P('dp', None, 'tp'), may hold values from -12 to 12
- query_rope: bfloat16 [128, 3, 1024], P('dp', None, 'tp'), may hold values from -120 to 120
- key_absorb: bfloat16 [16, 128, 512], P('tp'), may hold values from -0.5 to 0.5
- value_up: bfloat16 [16, 512, 128], P('tp'), may hold values from -0.25 to 0.25
- cache: bfloat16 [128, 128, 576], P('dp'), may hold values from -6 to 6
- cache_len: int32 [128], P('dp'), may hold values from 1 to 128, as said below
- counts: int32 [16], P('dp'), may hold values from 1 to 8, as said below
Outputs:
- attended: bfloat16 [128, 3, 2048], P('dp', None, 'tp')
The draws below stay inside these ranges and needn't reach their ends.
Inputs may be any that keep to these rules, and one draw needn't show every extreme that they name: `cache_len`: each sample's cache holds valid rows first. `counts`: a replica's live samples are its first slots.
All inputs are finite; a program needn't handle non-finite values.
Results may differ from the reference program's by a relative error of at most 0.011.
Values may be sent and summed in bfloat16 or wider, within the bound.
A program may use at most 64 MiB of HBM per device.

```python
import jax
import jax.numpy as jnp
from jax import lax

D = 7168
LAT = 512
ROPE = 64
NOPE = 128
VDIM = 128
PREFIX = 1024
SLOTS = 8
STEPS = 3
CTX = 128
HEADS = 16
SAMPLES = 128
REPLICAS = 16


def draw_query_rope(key, part):
    key = jax.random.fold_in(key, 11)
    shape_key = jax.random.fold_in(key, 0)
    values = 2.0 * jax.random.normal(shape_key, (SAMPLES, STEPS, HEADS, ROPE), jnp.float32)
    values = jnp.clip(values, -12.0, 12.0)
    return values.reshape(SAMPLES, STEPS, HEADS * ROPE).astype(jnp.bfloat16)


def draw_cache_len(key, part):
    key = jax.random.fold_in(key, 23)
    first_key, second_key = jax.random.split(key)
    lengths = jax.random.randint(first_key, (SAMPLES,), 1, CTX + 1)
    chosen = jax.random.randint(second_key, (), 0, SAMPLES)
    return jnp.where(jnp.arange(SAMPLES) == chosen, CTX, lengths).astype(jnp.int32)


def draw_counts(key, part):
    key = jax.random.fold_in(key, 37)
    first_key, second_key = jax.random.split(key)
    numbers = jax.random.randint(first_key, (REPLICAS,), 1, SLOTS + 1)
    chosen = jax.random.randint(second_key, (), 0, REPLICAS)
    return jnp.where(jnp.arange(REPLICAS) == chosen, SLOTS, numbers).astype(jnp.int32)


def block_levels(stream_key, dims, cuts, smallest, largest):
    def one(dim, shards_of):
        draws = jax.random.uniform(jax.random.fold_in(jax.random.fold_in(stream_key, 6), dim), (shards_of,), jnp.float32, smallest / len(cuts), largest / len(cuts))
        return jnp.repeat(jnp.exp(draws), dims[dim] // shards_of).reshape((-1,) + (1,) * (len(dims) - dim - 1))

    level = one(*cuts[0])
    for cut in cuts[1:]:
        level = level * one(*cut)
    return level


def bell_draw(key, extent, spread, most, pieces=(), kind=jnp.bfloat16):
    result = jax.random.normal(key, extent, jnp.float32) * spread
    if len(pieces) > 0:
        result = block_levels(key, extent, pieces, -0.22, 0.18) * result
    return jnp.clip(result, min=-most, max=most).astype(kind)


def setup_inputs(seed: int = 0) -> dict:
    key_of = jax.random.split(jax.random.key(seed), 12)
    prefix_hidden = bell_draw(key_of[0], (PREFIX, D), 1.0, 6.0, ((0, 16), (1, 2)))
    down_kv = bell_draw(key_of[1], (D, LAT + ROPE), D ** -0.5, 0.0625, ((0, 2),))
    latent_gain = jnp.clip(1.0 + 0.18 * jax.random.normal(key_of[2], (LAT,), jnp.float32), 0.1, 1.9)
    step_hidden = bell_draw(key_of[3], (SAMPLES, STEPS, D), 1.0, 6.0, ((0, 16), (2, 2)))
    query_nope = bell_draw(key_of[4], (SAMPLES, STEPS, HEADS * NOPE), 2.0, 12.0, ((0, 16), (2, 2)))
    query_rope = draw_query_rope(jax.random.fold_in(key_of[11], 71), 0)
    key_absorb = bell_draw(key_of[6], (HEADS, NOPE, LAT), NOPE ** -0.5, 0.5, ((0, 2),))
    value_up = bell_draw(key_of[7], (HEADS, LAT, VDIM), LAT ** -0.5, 0.25, ((0, 2),))
    cache = bell_draw(key_of[8], (SAMPLES, CTX, LAT + ROPE), 1.0, 6.0, ((0, 16),))
    cache_len = draw_cache_len(jax.random.fold_in(key_of[11], 71), 0)
    counts = draw_counts(jax.random.fold_in(key_of[11], 71), 0)
    return dict(prefix_hidden=prefix_hidden, down_kv=down_kv, latent_gain=latent_gain, step_hidden=step_hidden, query_nope=query_nope, query_rope=query_rope, key_absorb=key_absorb, value_up=value_up, cache=cache, cache_len=cache_len, counts=counts)


def apply_rotary_embedding(values, positions):
    half_width = values.shape[-1] // 2
    frequencies = 10000.0 ** (-jnp.arange(half_width, dtype=jnp.float32) / half_width)
    angles = positions[..., None] * frequencies
    cosine = jnp.cos(angles)
    sine_part = jnp.sin(angles)
    first_half = values[..., :half_width]
    second_half = values[..., half_width:]
    return jnp.concatenate([first_half * cosine - second_half * sine_part, first_half * sine_part + second_half * cosine], axis=-1)

def finish(raw_rows, gain, positions):
    latent_width = gain.shape[0]
    latent = raw_rows[..., :latent_width]
    factor = lax.rsqrt(lax.optimization_barrier(jnp.mean(latent * latent, axis=-1, keepdims=True)) + 1e-06)
    normed = latent * factor * gain
    return jnp.concatenate([normed, apply_rotary_embedding(raw_rows[..., latent_width:], positions)], axis=-1).astype(jnp.bfloat16)

def reference(prefix_hidden, down_kv, latent_gain, step_hidden, query_nope, query_rope, key_absorb, value_up, cache, cache_len, counts):
    key_width = LAT + ROPE
    prefix_raw = jnp.dot(prefix_hidden, down_kv, preferred_element_type=jnp.float32)
    prefix_keys = finish(prefix_raw, latent_gain, jnp.arange(PREFIX, dtype=jnp.int32).astype(jnp.float32))
    step_unprojected = jnp.dot(step_hidden.reshape(SAMPLES * STEPS, D), down_kv, preferred_element_type=jnp.float32).reshape(SAMPLES, STEPS, key_width)
    step_ids = jnp.arange(STEPS, dtype=jnp.int32)
    new_pos = (PREFIX + cache_len[:, None] + step_ids[None, :]).astype(jnp.float32)
    new_keys = finish(step_unprojected, latent_gain, new_pos)
    nope_rows = query_nope.reshape(SAMPLES, STEPS, HEADS, NOPE).astype(jnp.float32)
    query_latent = jnp.einsum('stha,hal->sthl', nope_rows, key_absorb.astype(jnp.float32)).astype(jnp.bfloat16)
    query_rot = apply_rotary_embedding(query_rope.reshape(SAMPLES, STEPS, HEADS, ROPE).astype(jnp.float32), new_pos[:, :, None]).astype(jnp.bfloat16)
    queries = jnp.concatenate([query_latent, query_rot], axis=-1)
    logit_scale = (NOPE + ROPE) ** (-0.5)
    new_ok = step_ids[None, :] <= step_ids[:, None]

    def per_sample(sample):
        key_entries = jnp.concatenate([prefix_keys, cache[sample], new_keys[sample]], axis=0)
        query_entries = queries[sample].reshape(STEPS * HEADS, key_width)
        scores = jnp.dot(query_entries, key_entries.T, preferred_element_type=jnp.float32) * logit_scale
        cache_ok = jnp.arange(CTX, dtype=jnp.int32)[None, :] < cache_len[sample]
        is_valid = jnp.concatenate([jnp.ones((STEPS, PREFIX), bool), jnp.broadcast_to(cache_ok, (STEPS, CTX)), new_ok], axis=1)
        is_valid = jnp.repeat(is_valid, HEADS, axis=0)
        row_max = lax.optimization_barrier(jnp.max(jnp.where(is_valid, scores, -1e+30), axis=1, keepdims=True))
        weights = jnp.where(is_valid, jnp.exp(scores - row_max), 0.0)
        mixed_out = jnp.dot(weights, key_entries[:, :LAT].astype(jnp.float32), precision=lax.Precision.HIGHEST) / lax.optimization_barrier(jnp.sum(weights, axis=1, keepdims=True))
        return mixed_out.astype(jnp.bfloat16).reshape(STEPS, HEADS, LAT)
    latent_out = lax.map(per_sample, jnp.arange(SAMPLES, dtype=jnp.int32))
    projected = jnp.einsum('sthl,hlv->sthv', latent_out.astype(jnp.float32), value_up.astype(jnp.float32))
    is_live = jnp.arange(SAMPLES, dtype=jnp.int32) % SLOTS < jnp.repeat(counts, SLOTS)
    projected = jnp.where(is_live[:, None, None, None], projected, 0.0)
    return projected.reshape(SAMPLES, STEPS, HEADS * VDIM).astype(jnp.bfloat16)
```

```python
import functools

import jax
import jax.numpy as jnp
from jax import lax
from jax.experimental import pallas as pl
from jax.experimental.pallas import tpu as pltpu
from jax.sharding import PartitionSpec as P

PREFIX = 1024
MESH = pl.DeviceIdType.MESH
NEG = -1e30
LOG2E = 1.4426950408889634


def apply_rotary_embedding(values, positions):
    half_width = values.shape[-1] // 2
    frequencies = 10000.0 ** (-jnp.arange(half_width, dtype=jnp.float32) / half_width)
    angles = positions[..., None] * frequencies
    cosine = jnp.cos(angles)
    sine_part = jnp.sin(angles)
    first_half = values[..., :half_width]
    second_half = values[..., half_width:]
    return jnp.concatenate(
        [
            first_half * cosine - second_half * sine_part,
            first_half * sine_part + second_half * cosine,
        ],
        axis=-1,
    )


def finish(raw_rows, gain, positions):
    latent_width = gain.shape[0]
    latent = raw_rows[..., :latent_width]
    factor = lax.rsqrt(jnp.mean(latent * latent, axis=-1, keepdims=True) + 1e-06)
    normed = latent * factor * gain
    return jnp.concatenate(
        [normed, apply_rotary_embedding(raw_rows[..., latent_width:], positions)], axis=-1
    ).astype(jnp.bfloat16)


def own_keys(
    query_entries,
    key_entries,
    lengths,
    row_max,
    row_mass,
    row_total,
    attention_head_count,
    logit_scale,
    latent_width,
):
    total_keys = key_entries.shape[1]
    context = total_keys - query_entries.shape[1] // attention_head_count
    scores = (
        jnp.einsum("aru,aeu->are", query_entries, key_entries, preferred_element_type=jnp.float32)
        * logit_scale
    )
    key_ids = jnp.arange(total_keys, dtype=jnp.int32)
    row_step = jnp.arange(query_entries.shape[1], dtype=jnp.int32) // attention_head_count
    new_ok = (key_ids[None, :] >= context) & (key_ids[None, :] - context <= row_step[:, None])
    is_valid = (key_ids[None, None, :] < lengths[:, None, None]) | new_ok[None]
    new_max = jnp.maximum(
        row_max, jnp.max(jnp.where(is_valid, scores, -1e30), axis=2, keepdims=True)
    )
    weights = jnp.where(is_valid, jnp.exp(scores - new_max), 0.0)
    shrink = jnp.exp(row_max - new_max)
    row_mass = row_mass * shrink + jnp.sum(weights, axis=2, keepdims=True)
    row_total = row_total * shrink + jnp.einsum(
        "dev,dva->dea",
        weights,
        key_entries[..., :latent_width].astype(jnp.float32),
        precision=lax.Precision.HIGHEST,
    )
    return (row_total / row_mass).astype(jnp.bfloat16)


def local(
    prefix_hidden,
    down_kv,
    latent_gain,
    step_hidden,
    query_nope,
    query_rope,
    key_absorb,
    value_up,
    cache,
    cache_len,
    counts,
):
    key_width = down_kv.shape[1]
    latent_width = latent_gain.shape[0]
    slot_count, step_count, _ = step_hidden.shape
    attention_head_count, nope_width, _ = key_absorb.shape
    rope_width = key_width - latent_width
    logit_scale = (nope_width + rope_width) ** (-0.5)
    partial_rows = jnp.dot(prefix_hidden, down_kv, preferred_element_type=jnp.float32)
    step_part = jnp.dot(
        step_hidden.reshape(slot_count * step_count, -1),
        down_kv,
        preferred_element_type=jnp.float32,
    )
    step_unprojected = lax.psum(step_part, "tp").reshape(slot_count, step_count, key_width)
    step_ids = jnp.arange(step_count, dtype=jnp.int32)
    new_pos = (PREFIX + cache_len[:, None] + step_ids[None, :]).astype(jnp.float32)
    new_keys = finish(step_unprojected, latent_gain, new_pos)
    nope_rows = query_nope.reshape(slot_count, step_count, attention_head_count, nope_width)
    query_latent = jnp.einsum(
        "stha,hal->sthl", nope_rows, key_absorb, preferred_element_type=jnp.float32
    ).astype(jnp.bfloat16)
    query_rot = apply_rotary_embedding(
        query_rope.reshape(slot_count, step_count, attention_head_count, rope_width).astype(
            jnp.float32
        ),
        new_pos[:, :, None],
    ).astype(jnp.bfloat16)
    queries = jnp.concatenate([query_latent, query_rot], axis=-1).reshape(
        slot_count * step_count * attention_head_count, key_width
    )
    total_rows = queries.shape[0]
    block_rows = partial_rows.shape[0]
    common_prompt_rows = lax.psum_scatter(partial_rows, "tp", scatter_dimension=0, tiled=True)
    share_count = common_prompt_rows.shape[0]
    first_row = lax.axis_index("dp") * block_rows + lax.axis_index("tp") * share_count
    positions = (first_row + jnp.arange(share_count, dtype=jnp.int32)).astype(jnp.float32)
    prefix_keys = finish(common_prompt_rows, latent_gain, positions)
    key_piece = lax.all_gather(prefix_keys, ("dp", "tp"), axis=0, tiled=True)
    row_max = jnp.full((total_rows, 1), -1e30, jnp.float32)
    scores = (
        jnp.einsum("qc,kc->qk", queries, key_piece, preferred_element_type=jnp.float32)
        * logit_scale
    )
    new_max = jnp.maximum(row_max, jnp.max(scores, axis=1, keepdims=True))
    weights = jnp.exp(scores - new_max)
    row_mass = jnp.sum(weights, axis=1, keepdims=True)
    row_total = jnp.dot(
        weights, key_piece[:, :latent_width].astype(jnp.float32), precision=lax.Precision.HIGHEST
    )
    row_max, row_mass, row_total = (new_max, row_mass, row_total)
    per_slot = step_count * attention_head_count
    query_slots = queries.reshape(slot_count, per_slot, key_width)
    row_max = row_max.reshape(slot_count, per_slot, 1)
    row_mass = row_mass.reshape(slot_count, per_slot, 1)
    row_total = row_total.reshape(slot_count, per_slot, latent_width)
    key_entries = jnp.concatenate([cache, new_keys], axis=1)
    live_count = counts[0]
    is_live = jnp.arange(slot_count, dtype=jnp.int32) < live_count
    latent_out = own_keys(
        query_slots,
        key_entries,
        cache_len,
        row_max,
        row_mass,
        row_total,
        attention_head_count,
        logit_scale,
        latent_width,
    )
    latent_out = latent_out.reshape(slot_count, step_count, attention_head_count, latent_width)
    projected = jnp.einsum(
        "sthl,hlv->sthv", latent_out, value_up, preferred_element_type=jnp.float32
    )
    projected = jnp.where(is_live[:, None, None, None], projected, 0.0)
    return projected.reshape(slot_count, step_count, -1).astype(jnp.bfloat16)


def rotate(x, cosine, signed_sine):
    lane = lax.broadcasted_iota(jnp.int32, x.shape, 1) % 64
    swapped = jnp.where(lane < 32, pltpu.roll(x, 96, 1), pltpu.roll(x, 32, 1))
    return x * cosine + swapped * signed_sine


def fused_kernel(
    prefix_hbm,
    step_hbm,
    down_hbm,
    nope_ref,
    rope_ref,
    absorb_hbm,
    value_hbm,
    cache_hbm,
    gain_ref,
    cos_ref,
    sin_ref,
    bias_ref,
    out_ref,
    hidden,
    down,
    absorb,
    value,
    own,
    keys,
    queries,
    partial,
    arrived,
    load_sem,
    pair_send,
    pair_recv,
    send_sem,
    z_recv,
    x_recv,
    y_recv,
    d1_recv,
    d2_recv,
    s_recv,
    *,
    chunks,
    logit_scale,
):
    dp = lax.axis_index("dp")
    tp = lax.axis_index("tp")
    z, y, x = dp // 4, (dp // 2) % 2, dp % 2
    latent = gain_ref.shape[1]
    width = keys.shape[1]
    heads = absorb.shape[0]
    nope = absorb.shape[1]
    share = 32
    rows = 32

    def place(zz, yy, xx):
        return zz * 4 + yy * 2 + xx

    def zof(shift):
        return lax.rem(z + shift + 4, 4)

    x_dev = (place(z, y, 1 - x), tp)
    y_dev = (place(z, 1 - y, x), tp)
    sib_dev = (dp, 1 - tp)
    z_devs = {d: (place(zof(d), y, x), tp) for d in (1, 2, 3)}

    barrier = pltpu.get_barrier_semaphore()
    for dev in (x_dev, y_dev, sib_dev, z_devs[1], z_devs[2], z_devs[3]):
        pl.semaphore_signal(barrier, inc=1, device_id=dev, device_id_type=MESH)

    prefix_rows = prefix_hbm.shape[0]
    depth = down_hbm.shape[0] // chunks
    loads = []

    def load(src, dst, i):
        copy = pltpu.make_async_copy(src, dst, load_sem.at[i])
        copy.start()
        return copy

    hid_a = load(prefix_hbm, hidden.at[pl.ds(0, prefix_rows), :], 0)
    hid_b = load(step_hbm, hidden.at[pl.ds(prefix_rows, rows), :], 1)
    for i in range(chunks):
        span = pl.ds(i * depth, depth)
        loads.append(load(down_hbm.at[span, :], down.at[span, :], 2 + i))
    ab_load = load(absorb_hbm, absorb, 2 + chunks)
    ca_load = load(cache_hbm, own.at[pl.ds(0, cache_hbm.shape[0]), :], 3 + chunks)
    va_load = load(value_hbm, value, 4 + chunks)

    hid_a.wait()
    hid_b.wait()
    total = None
    for i in range(chunks):
        loads[i].wait()
        part = jnp.dot(
            hidden[:, i * depth : (i + 1) * depth],
            down[i * depth : (i + 1) * depth, :],
            preferred_element_type=jnp.float32,
        )
        total = part if total is None else total + part
    partial[...] = total

    pl.semaphore_wait(barrier, 6)
    theirs = pl.ds(pl.multiple_of((1 - tp) * share, share), share)
    mine = pl.ds(pl.multiple_of(tp * share, share), share)

    def remote(src, dst, ssem, rsem, dev):
        return pltpu.make_async_remote_copy(
            src_ref=src, dst_ref=dst, send_sem=ssem, recv_sem=rsem, device_id=dev, device_id_type=MESH
        )

    pair_a = remote(
        partial.at[theirs, :], arrived.at[pl.ds(0, share), :], pair_send.at[0], pair_recv.at[0], sib_dev
    )
    pair_b = remote(
        partial.at[pl.ds(prefix_rows, rows), :],
        arrived.at[pl.ds(share, rows), :],
        pair_send.at[1],
        pair_recv.at[1],
        sib_dev,
    )
    pair_a.start()
    pair_b.start()

    def finished(raw, at):
        low = raw[:, :latent]
        factor = lax.rsqrt(jnp.mean(low * low, axis=1, keepdims=True) + 1e-06)
        rope = raw[:, latent:]
        both = jnp.concatenate([rope, rope], axis=1)
        turned = rotate(both, cos_ref[at : at + rows, :], sin_ref[at : at + rows, :])
        return (low * factor * gain_ref[...]).astype(jnp.bfloat16), turned[:, : width - latent].astype(
            jnp.bfloat16
        )

    pair_a.wait_recv()
    low, high = finished(partial[mine, :] + arrived[0:share, :], 0)

    def block(core, zz, yy, xx):
        return pl.multiple_of((core * 16 + place(zz, yy, xx)) * share, share)

    my_block = pl.ds(block(tp, z, y, x), share)
    keys[my_block, :latent] = low
    keys[my_block, latent:] = high

    sends = []

    def send(start, size, rsem, dev):
        ref = keys.at[pl.ds(start, size), :]
        copy = remote(ref, ref, send_sem.at[len(sends)], rsem, dev)
        copy.start()
        sends.append(copy)

    def await_block(start, size, rsem, dev):
        ref = keys.at[pl.ds(start, size), :]
        remote(ref, ref, send_sem.at[0], rsem, dev).wait_recv()

    start = block(tp, z, y, x)
    for d in (2, 1, 3):
        send(start, share, z_recv.at[d], z_devs[d])
    send(start, share, x_recv.at[0], x_dev)
    send(start, share, y_recv.at[0], y_dev)
    send(start, share, s_recv.at[0], sib_dev)

    ab_load.wait()
    for h in range(heads):
        ql = jnp.dot(
            nope_ref[:, h * nope : (h + 1) * nope], absorb[h], preferred_element_type=jnp.float32
        )
        queries[h * rows : (h + 1) * rows, :latent] = ql.astype(jnp.bfloat16)
    for p in range(heads // 2):
        turned = rotate(
            rope_ref[:, p * 128 : (p + 1) * 128].astype(jnp.float32),
            cos_ref[rows : 2 * rows, :],
            sin_ref[rows : 2 * rows, :],
        ).astype(jnp.bfloat16)
        queries[2 * p * rows : (2 * p + 1) * rows, latent:] = turned[:, :64]
        queries[(2 * p + 1) * rows : (2 * p + 2) * rows, latent:] = turned[:, 64:]

    for d in (1, 3, 2):
        zs = zof(-d)
        start = block(tp, zs, y, x)
        await_block(start, share, z_recv.at[d], z_devs[d])
        send(start, share, x_recv.at[d], x_dev)
        send(start, share, y_recv.at[d], y_dev)
        send(start, share, s_recv.at[d], sib_dev)

    def forward(d):
        zs = zof(-d)
        start = block(tp, zs, y, 1 - x)
        await_block(start, share, x_recv.at[d], x_dev)
        send(start, share // 2, d1_recv.at[d], y_dev)
        send(start, share, s_recv.at[4 + d], sib_dev)
        start = block(tp, zs, 1 - y, x)
        await_block(start, share, y_recv.at[d], y_dev)
        send(start + share // 2, share // 2, d2_recv.at[d], x_dev)
        send(start, share, s_recv.at[8 + d], sib_dev)

    forward(0)

    ctx = cache_hbm.shape[0]
    pair_b.wait_recv()
    low, high = finished(partial[prefix_rows:, :] + arrived[share:, :], rows)
    own[ctx : ctx + rows, :latent] = low
    own[ctx : ctx + rows, latent:] = high
    own[ctx + rows :, :] = jnp.zeros((own.shape[0] - ctx - rows, width), jnp.bfloat16)
    ca_load.wait()
    q = queries[...]
    factor = logit_scale * LOG2E
    nt = (((1,), (1,)), ((), ()))
    s_own = lax.dot_general(q, own[...], nt, preferred_element_type=jnp.float32)
    s_own = (s_own.reshape(heads, rows, -1) + bias_ref[...][None]).reshape(heads * rows, -1)
    m_own = jnp.max(s_own, axis=1, keepdims=True)

    for d in (1, 3, 2):
        forward(d)

    p_own = jnp.exp2((s_own - m_own) * factor)
    l_own = jnp.sum(p_own, axis=1, keepdims=True)
    o_own = jnp.dot(
        p_own.astype(jnp.bfloat16), own[:, :latent], preferred_element_type=jnp.float32
    )

    for d in (0, 1, 3, 2):
        start = block(tp, zof(-d), 1 - y, 1 - x)
        await_block(start, share // 2, d1_recv.at[d], y_dev)
        await_block(start + share // 2, share // 2, d2_recv.at[d], x_dev)
        send(start, share, s_recv.at[12 + d], sib_dev)

    for d in (0, 1, 3, 2):
        zs = zof(-d)
        await_block(block(1 - tp, zs, y, x), share, s_recv.at[d], sib_dev)
        await_block(block(1 - tp, zs, y, 1 - x), share, s_recv.at[4 + d], sib_dev)
        await_block(block(1 - tp, zs, 1 - y, x), share, s_recv.at[8 + d], sib_dev)
        await_block(block(1 - tp, zs, 1 - y, 1 - x), share, s_recv.at[12 + d], sib_dev)

    va_load.wait()
    s_all = lax.dot_general(q, keys[...], nt, preferred_element_type=jnp.float32)
    m_all = jnp.maximum(m_own, jnp.max(s_all, axis=1, keepdims=True))
    p_all = jnp.exp2((s_all - m_all) * factor)
    shrink = jnp.exp2((m_own - m_all) * factor)
    mass = jnp.sum(p_all, axis=1, keepdims=True) + l_own * shrink
    mixed = jnp.dot(p_all.astype(jnp.bfloat16), keys[:, :latent], preferred_element_type=jnp.float32)
    mixed = ((mixed + o_own * shrink) / mass).astype(jnp.bfloat16)
    vdim = value.shape[2]
    for h in range(heads):
        out_ref[:, h * vdim : (h + 1) * vdim] = jnp.dot(
            mixed[h * rows : (h + 1) * rows, :], value[h], preferred_element_type=jnp.float32
        ).astype(jnp.bfloat16)

    pair_a.wait_send()
    pair_b.wait_send()
    for copy in sends:
        copy.wait_send()


def local_fused(
    prefix_hidden,
    down_kv,
    latent_gain,
    step_hidden,
    query_nope,
    query_rope,
    key_absorb,
    value_up,
    cache,
    cache_len,
    counts,
):
    key_width = down_kv.shape[1]
    latent_width = latent_gain.shape[0]
    slots, steps, _ = step_hidden.shape
    heads, nope_width, _ = key_absorb.shape
    vdim = value_up.shape[2]
    rope_width = key_width - latent_width
    logit_scale = (nope_width + rope_width) ** (-0.5)
    context = cache.shape[1]
    rows = slots * 4
    own_rows = slots * context + 128
    block_rows = prefix_hidden.shape[0]
    share = block_rows // 2

    def four(values):
        return jnp.pad(values, ((0, 0), (0, 4 - steps), (0, 0))).reshape(rows, -1)

    first = lax.axis_index("dp") * block_rows + lax.axis_index("tp") * share
    step_ids = jnp.arange(4, dtype=jnp.int32)
    new_pos = (PREFIX + cache_len[:, None] + step_ids[None, :]).reshape(rows)
    positions = jnp.concatenate([first + jnp.arange(share, dtype=jnp.int32), new_pos])
    lane = jnp.arange(128, dtype=jnp.int32)
    half = rope_width // 2
    frequencies = 10000.0 ** (-(lane % half).astype(jnp.float32) / half)
    angles = positions.astype(jnp.float32)[:, None] * frequencies[None, :]
    cosine = jnp.cos(angles)
    signed_sine = jnp.where(lane[None, :] % rope_width < half, -1.0, 1.0) * jnp.sin(angles)

    row = jnp.arange(rows, dtype=jnp.int32)[:, None]
    col = jnp.arange(own_rows, dtype=jnp.int32)[None, :]
    limit = jnp.repeat(cache_len, 4)[:, None]
    in_cache = (col < slots * context) & (col // context == row // 4) & (col % context < limit)
    fresh = col - slots * context
    in_new = (fresh >= 0) & (fresh // 4 == row // 4) & (fresh % 4 <= row % 4)
    bias = jnp.where(in_cache | in_new, 0.0, NEG)

    chunks = 7
    vmem = pl.BlockSpec(memory_space=pltpu.VMEM)
    anyw = pl.BlockSpec(memory_space=pl.ANY)
    dma = pltpu.SemaphoreType.DMA
    bf = jnp.bfloat16
    out = pl.pallas_call(
        functools.partial(fused_kernel, chunks=chunks, logit_scale=logit_scale),
        out_shape=jax.ShapeDtypeStruct((rows, heads * vdim), bf),
        in_specs=[anyw, anyw, anyw, vmem, vmem, anyw, anyw, anyw, vmem, vmem, vmem, vmem],
        out_specs=vmem,
        scratch_shapes=[
            pltpu.VMEM((block_rows + rows, prefix_hidden.shape[1]), bf),
            pltpu.VMEM(down_kv.shape, bf),
            pltpu.VMEM(key_absorb.shape, bf),
            pltpu.VMEM(value_up.shape, bf),
            pltpu.VMEM((own_rows, key_width), bf),
            pltpu.VMEM((PREFIX, key_width), bf),
            pltpu.VMEM((heads * rows, key_width), bf),
            pltpu.VMEM((block_rows + rows, key_width), jnp.float32),
            pltpu.VMEM((share + rows, key_width), jnp.float32),
            dma((5 + chunks,)),
            dma((2,)),
            dma((2,)),
            dma((40,)),
            dma((4,)),
            dma((4,)),
            dma((4,)),
            dma((4,)),
            dma((4,)),
            dma((16,)),
        ],
        compiler_params=pltpu.CompilerParams(
            collective_id=0, has_side_effects=True, vmem_limit_bytes=48 * 1024 * 1024
        ),
    )(
        prefix_hidden,
        four(step_hidden),
        down_kv,
        four(query_nope),
        four(query_rope),
        key_absorb,
        value_up,
        cache.reshape(slots * context, key_width),
        latent_gain[None, :],
        cosine,
        signed_sine,
        bias,
    )
    is_live = jnp.arange(slots, dtype=jnp.int32) < counts[0]
    out = out.reshape(slots, 4, heads * vdim)[:, :steps]
    return jnp.where(is_live[:, None, None], out, jnp.zeros((), bf))


def solution(mesh):
    in_specs = (
        P("dp", "tp"),
        P("tp", None),
        P(),
        P("dp", None, "tp"),
        P("dp", None, "tp"),
        P("dp", None, "tp"),
        P("tp", None, None),
        P("tp", None, None),
        P("dp", None, None),
        P("dp"),
        P("dp"),
    )
    out_specs = P("dp", None, "tp")
    fused = mesh.shape["dp"] == 16 and mesh.shape["tp"] == 2
    return jax.shard_map(local_fused if fused else local, mesh=mesh, in_specs=in_specs, out_specs=out_specs, check_vma=False)
```

```python
import functools

import jax
import jax.numpy as jnp
from jax import lax
from jax.experimental import pallas as pl
from jax.experimental.pallas import tpu as pltpu
from jax.sharding import PartitionSpec as P

PREFIX = 1024
MESH = pl.DeviceIdType.MESH
NEG = -1e30
LOG2E = 1.4426950408889634
LOG1E4 = 9.210340371976184


def apply_rotary_embedding(values, positions):
    half_width = values.shape[-1] // 2
    frequencies = 10000.0 ** (-jnp.arange(half_width, dtype=jnp.float32) / half_width)
    angles = positions[..., None] * frequencies
    cosine = jnp.cos(angles)
    sine_part = jnp.sin(angles)
    first_half = values[..., :half_width]
    second_half = values[..., half_width:]
    return jnp.concatenate(
        [
            first_half * cosine - second_half * sine_part,
            first_half * sine_part + second_half * cosine,
        ],
        axis=-1,
    )


def finish(raw_rows, gain, positions):
    latent_width = gain.shape[0]
    latent = raw_rows[..., :latent_width]
    factor = lax.rsqrt(jnp.mean(latent * latent, axis=-1, keepdims=True) + 1e-06)
    normed = latent * factor * gain
    return jnp.concatenate(
        [normed, apply_rotary_embedding(raw_rows[..., latent_width:], positions)], axis=-1
    ).astype(jnp.bfloat16)


def own_keys(
    query_entries,
    key_entries,
    lengths,
    row_max,
    row_mass,
    row_total,
    attention_head_count,
    logit_scale,
    latent_width,
):
    total_keys = key_entries.shape[1]
    context = total_keys - query_entries.shape[1] // attention_head_count
    scores = (
        jnp.einsum("aru,aeu->are", query_entries, key_entries, preferred_element_type=jnp.float32)
        * logit_scale
    )
    key_ids = jnp.arange(total_keys, dtype=jnp.int32)
    row_step = jnp.arange(query_entries.shape[1], dtype=jnp.int32) // attention_head_count
    new_ok = (key_ids[None, :] >= context) & (key_ids[None, :] - context <= row_step[:, None])
    is_valid = (key_ids[None, None, :] < lengths[:, None, None]) | new_ok[None]
    new_max = jnp.maximum(
        row_max, jnp.max(jnp.where(is_valid, scores, -1e30), axis=2, keepdims=True)
    )
    weights = jnp.where(is_valid, jnp.exp(scores - new_max), 0.0)
    shrink = jnp.exp(row_max - new_max)
    row_mass = row_mass * shrink + jnp.sum(weights, axis=2, keepdims=True)
    row_total = row_total * shrink + jnp.einsum(
        "dev,dva->dea",
        weights,
        key_entries[..., :latent_width].astype(jnp.float32),
        precision=lax.Precision.HIGHEST,
    )
    return (row_total / row_mass).astype(jnp.bfloat16)


def local(
    prefix_hidden,
    down_kv,
    latent_gain,
    step_hidden,
    query_nope,
    query_rope,
    key_absorb,
    value_up,
    cache,
    cache_len,
    counts,
):
    key_width = down_kv.shape[1]
    latent_width = latent_gain.shape[0]
    slot_count, step_count, _ = step_hidden.shape
    attention_head_count, nope_width, _ = key_absorb.shape
    rope_width = key_width - latent_width
    logit_scale = (nope_width + rope_width) ** (-0.5)
    partial_rows = jnp.dot(prefix_hidden, down_kv, preferred_element_type=jnp.float32)
    step_part = jnp.dot(
        step_hidden.reshape(slot_count * step_count, -1),
        down_kv,
        preferred_element_type=jnp.float32,
    )
    step_unprojected = lax.psum(step_part, "tp").reshape(slot_count, step_count, key_width)
    step_ids = jnp.arange(step_count, dtype=jnp.int32)
    new_pos = (PREFIX + cache_len[:, None] + step_ids[None, :]).astype(jnp.float32)
    new_keys = finish(step_unprojected, latent_gain, new_pos)
    nope_rows = query_nope.reshape(slot_count, step_count, attention_head_count, nope_width)
    query_latent = jnp.einsum(
        "stha,hal->sthl", nope_rows, key_absorb, preferred_element_type=jnp.float32
    ).astype(jnp.bfloat16)
    query_rot = apply_rotary_embedding(
        query_rope.reshape(slot_count, step_count, attention_head_count, rope_width).astype(
            jnp.float32
        ),
        new_pos[:, :, None],
    ).astype(jnp.bfloat16)
    queries = jnp.concatenate([query_latent, query_rot], axis=-1).reshape(
        slot_count * step_count * attention_head_count, key_width
    )
    total_rows = queries.shape[0]
    block_rows = partial_rows.shape[0]
    common_prompt_rows = lax.psum_scatter(partial_rows, "tp", scatter_dimension=0, tiled=True)
    share_count = common_prompt_rows.shape[0]
    first_row = lax.axis_index("dp") * block_rows + lax.axis_index("tp") * share_count
    positions = (first_row + jnp.arange(share_count, dtype=jnp.int32)).astype(jnp.float32)
    prefix_keys = finish(common_prompt_rows, latent_gain, positions)
    key_piece = lax.all_gather(prefix_keys, ("dp", "tp"), axis=0, tiled=True)
    row_max = jnp.full((total_rows, 1), -1e30, jnp.float32)
    scores = (
        jnp.einsum("qc,kc->qk", queries, key_piece, preferred_element_type=jnp.float32)
        * logit_scale
    )
    new_max = jnp.maximum(row_max, jnp.max(scores, axis=1, keepdims=True))
    weights = jnp.exp(scores - new_max)
    row_mass = jnp.sum(weights, axis=1, keepdims=True)
    row_total = jnp.dot(
        weights, key_piece[:, :latent_width].astype(jnp.float32), precision=lax.Precision.HIGHEST
    )
    row_max, row_mass, row_total = (new_max, row_mass, row_total)
    per_slot = step_count * attention_head_count
    query_slots = queries.reshape(slot_count, per_slot, key_width)
    row_max = row_max.reshape(slot_count, per_slot, 1)
    row_mass = row_mass.reshape(slot_count, per_slot, 1)
    row_total = row_total.reshape(slot_count, per_slot, latent_width)
    key_entries = jnp.concatenate([cache, new_keys], axis=1)
    live_count = counts[0]
    is_live = jnp.arange(slot_count, dtype=jnp.int32) < live_count
    latent_out = own_keys(
        query_slots,
        key_entries,
        cache_len,
        row_max,
        row_mass,
        row_total,
        attention_head_count,
        logit_scale,
        latent_width,
    )
    latent_out = latent_out.reshape(slot_count, step_count, attention_head_count, latent_width)
    projected = jnp.einsum(
        "sthl,hlv->sthv", latent_out, value_up, preferred_element_type=jnp.float32
    )
    projected = jnp.where(is_live[:, None, None, None], projected, 0.0)
    return projected.reshape(slot_count, step_count, -1).astype(jnp.bfloat16)


def rotate(x, cosine, signed_sine):
    lane = lax.broadcasted_iota(jnp.int32, x.shape, 1) % 64
    swapped = jnp.where(lane < 32, pltpu.roll(x, 96, 1), pltpu.roll(x, 32, 1))
    return x * cosine + swapped * signed_sine


def fused_kernel(
    len_ref,
    count_ref,
    prefix_hbm,
    step_hbm,
    down_hbm,
    nope_hbm,
    rope_hbm,
    absorb_hbm,
    value_hbm,
    cache_hbm,
    gain_hbm,
    out_ref,
    hidden,
    step,
    down,
    nope_rows,
    rope_rows,
    absorb,
    value,
    cache,
    gain,
    fresh,
    keys,
    queries,
    partial,
    arrived,
    load_sem,
    pair_send,
    pair_recv,
    send_sem,
    z_recv,
    x_recv,
    y_recv,
    d1_recv,
    d2_recv,
    s_recv,
    *,
    chunks,
    logit_scale,
):
    dp = lax.axis_index("dp")
    tp = lax.axis_index("tp")
    z, y, x = dp // 4, (dp // 2) % 2, dp % 2
    latent = gain.shape[1]
    width = keys.shape[1]
    heads, nope, _ = absorb.shape
    slots, _, ctx = cache.shape
    share = 32
    rows = 32
    f32, bf = jnp.float32, jnp.bfloat16

    def place(zz, yy, xx):
        return zz * 4 + yy * 2 + xx

    x_dev = (place(z, y, 1 - x), tp)
    y_dev = (place(z, 1 - y, x), tp)
    sib_dev = (dp, 1 - tp)
    z_devs = {d: (place(lax.rem(z + d, 4), y, x), tp) for d in (1, 2, 3)}

    barrier = pltpu.get_barrier_semaphore()
    for dev in (x_dev, y_dev, sib_dev, z_devs[1], z_devs[2], z_devs[3]):
        pl.semaphore_signal(barrier, inc=1, device_id=dev, device_id_type=MESH)

    prefix_rows, model = prefix_hbm.shape
    depth = model // chunks

    def load(src, dst, i):
        copy = pltpu.make_async_copy(src, dst, load_sem.at[i])
        copy.start()
        return copy

    step_load = load(step_hbm, step, 0)
    prefix_load = load(prefix_hbm, hidden.at[pl.ds(0, prefix_rows), :], 1)
    down_loads = []
    for i in range(chunks):
        span = pl.ds(i * depth, depth)
        down_loads.append(load(down_hbm.at[:, span], down.at[:, span], 8 + i))
    nope_load = load(nope_hbm, nope_rows, 2)
    rope_load = load(rope_hbm, rope_rows, 3)
    absorb_load = load(absorb_hbm, absorb, 4)
    gain_load = load(gain_hbm, gain, 5)
    cache_load = load(cache_hbm, cache, 6)
    value_load = load(value_hbm, value, 7)

    def padded(value_rows):
        wide = value_rows.astype(f32)
        return jnp.concatenate([wide, jnp.zeros((rows - wide.shape[0], wide.shape[1]), f32)], axis=0)

    sub = lax.broadcasted_iota(jnp.int32, (8, 128), 0)
    lane = lax.broadcasted_iota(jnp.int32, (8, 128), 1)
    lens = jnp.zeros((8, 128), jnp.int32)
    for s in range(slots):
        lens = jnp.where(sub == s, len_ref[s], lens)
    half = (width - latent) // 2
    frequency = jnp.exp((lane % half).astype(f32) * (-LOG1E4 / half))
    first = dp * prefix_rows + tp * share
    sign = jnp.where(lane % (2 * half) < half, -1.0, 1.0)
    cosines, sines = [], []
    for g in range((share + rows) // 8):
        if g < share // 8:
            position = first + g * 8 + sub
        else:
            position = PREFIX + lens + (g - share // 8)
        angle = position.astype(f32) * frequency
        cosines.append(jnp.cos(angle))
        sines.append(jnp.sin(angle) * sign)
    key_cos = jnp.concatenate(cosines[: share // 8], axis=0)
    key_sin = jnp.concatenate(sines[: share // 8], axis=0)
    step_cos = jnp.concatenate(cosines[share // 8 :], axis=0)
    step_sin = jnp.concatenate(sines[share // 8 :], axis=0)

    nt = (((1,), (1,)), ((), ()))
    step_load.wait()
    hidden[prefix_rows:, :] = padded(step[...]).astype(bf)
    prefix_load.wait()
    total = None
    for i in range(chunks):
        down_loads[i].wait()
        part = lax.dot_general(
            hidden[:, i * depth : (i + 1) * depth],
            down[:, i * depth : (i + 1) * depth],
            nt,
            preferred_element_type=f32,
        )
        total = part if total is None else total + part
    partial[...] = total

    pl.semaphore_wait(barrier, 6)
    theirs = pl.ds(pl.multiple_of((1 - tp) * share, share), share)
    mine = pl.ds(pl.multiple_of(tp * share, share), share)

    def remote(src, dst, ssem, rsem, dev):
        return pltpu.make_async_remote_copy(
            src_ref=src, dst_ref=dst, send_sem=ssem, recv_sem=rsem, device_id=dev, device_id_type=MESH
        )

    pair_a = remote(
        partial.at[theirs, :], arrived.at[pl.ds(0, share), :], pair_send.at[0], pair_recv.at[0], sib_dev
    )
    pair_b = remote(
        partial.at[pl.ds(prefix_rows, rows), :],
        arrived.at[pl.ds(share, rows), :],
        pair_send.at[1],
        pair_recv.at[1],
        sib_dev,
    )
    pair_a.start()
    pair_b.start()

    nope_load.wait()
    absorb_load.wait()
    nopes = padded(nope_rows[...]).astype(bf)
    for h in range(heads):
        ql = jnp.dot(nopes[:, h * nope : (h + 1) * nope], absorb[h], preferred_element_type=f32)
        queries[h * rows : (h + 1) * rows, :latent] = ql.astype(bf)
    rope_load.wait()
    ropes = padded(rope_rows[...])
    for p in range(heads // 2):
        turned = rotate(ropes[:, p * 128 : (p + 1) * 128], step_cos, step_sin).astype(bf)
        queries[2 * p * rows : (2 * p + 1) * rows, latent:] = turned[:, :64]
        queries[(2 * p + 1) * rows : (2 * p + 2) * rows, latent:] = turned[:, 64:]
    gain_load.wait()

    def finished(raw, cosine, signed_sine):
        low = raw[:, :latent]
        factor = lax.rsqrt(jnp.mean(low * low, axis=1, keepdims=True) + 1e-06)
        rope = raw[:, latent:]
        turned = rotate(jnp.concatenate([rope, rope], axis=1), cosine, signed_sine)
        return (low * factor * gain[...]).astype(bf), turned[:, : width - latent].astype(bf)

    pair_a.wait_recv()
    low, high = finished(partial[mine, :] + arrived[0:share, :], key_cos, key_sin)

    def block(group, d):
        return (group * 4 + d) * share

    keys[0:share, :latent] = low
    keys[0:share, latent:] = high

    sends = []

    def send(source, target, size, rsem, dev):
        copy = remote(
            keys.at[pl.ds(source, size), :],
            keys.at[pl.ds(target, size), :],
            send_sem.at[len(sends)],
            rsem,
            dev,
        )
        copy.start()
        sends.append(copy)

    def await_block(start, size, rsem, dev):
        ref = keys.at[pl.ds(start, size), :]
        remote(ref, ref, send_sem.at[0], rsem, dev).wait_recv()

    def along(d):
        source = block(0, d)
        send(source, block(2, d), share, x_recv.at[d], x_dev)
        send(source, block(3, d), share, y_recv.at[d], y_dev)
        send(source, block(1, d), share, s_recv.at[d], sib_dev)

    for d in (2, 1, 3):
        send(0, block(0, d), share, z_recv.at[d], z_devs[d])
    along(0)

    pair_b.wait_recv()
    low, high = finished(partial[prefix_rows:, :] + arrived[share:, :], step_cos, step_sin)
    fresh[0:rows, :latent] = low
    fresh[0:rows, latent:] = high
    fresh[rows:, :] = jnp.zeros((fresh.shape[0] - rows, width), bf)

    for d in (1, 3, 2):
        await_block(block(0, d), share, z_recv.at[d], z_devs[d])
        along(d)

    cache_load.wait()
    q = queries[...]
    factor = logit_scale * LOG2E

    def own_scores(s):
        raw = jnp.dot(q, cache[s], preferred_element_type=f32).reshape(heads * rows // 8, 8, ctx)
        valid = (sub == s) & (lane < len_ref[s])
        return jnp.where(valid[None], raw, NEG).reshape(heads * rows, ctx)

    parts = [own_scores(s) for s in range(slots)]
    r32 = lax.broadcasted_iota(jnp.int32, (rows, 128), 0)
    c32 = lax.broadcasted_iota(jnp.int32, (rows, 128), 1)
    ok = (c32 % 8 == r32 % 8) & (c32 // 8 <= r32 // 8)
    raw = lax.dot_general(q, fresh[...], nt, preferred_element_type=f32).reshape(heads, rows, 128)
    parts.append(jnp.where(ok[None], raw, NEG).reshape(heads * rows, 128))

    def forward(d):
        source = block(2, d)
        await_block(source, share, x_recv.at[d], x_dev)
        send(source, block(6, d), share // 2, d1_recv.at[d], y_dev)
        send(source, block(4, d), share, s_recv.at[4 + d], sib_dev)
        source = block(3, d)
        await_block(source, share, y_recv.at[d], y_dev)
        send(source + share // 2, block(6, d) + share // 2, share // 2, d2_recv.at[d], x_dev)
        send(source, block(5, d), share, s_recv.at[8 + d], sib_dev)

    for d in (0, 1, 3, 2):
        forward(d)

    top = functools.reduce(jnp.maximum, parts)
    top = jnp.max(top, axis=1, keepdims=True)
    mass, mixed = None, None
    weights = [jnp.exp2((part - top) * factor) for part in parts]
    mass = jnp.sum(functools.reduce(jnp.add, weights), axis=1, keepdims=True)
    mixed = jnp.dot(weights[slots].astype(bf), fresh[:, :latent], preferred_element_type=f32)
    for s in range(slots):
        mixed += lax.dot_general(
            weights[s].astype(bf), cache[s, :latent, :], nt, preferred_element_type=f32
        )

    def absorb_keys(start, size, top, mass, mixed):
        scores = lax.dot_general(q, keys[start : start + size, :], nt, preferred_element_type=f32)
        higher = jnp.maximum(top, jnp.max(scores, axis=1, keepdims=True))
        weights = jnp.exp2((scores - higher) * factor)
        shrink = jnp.exp2((top - higher) * factor)
        mass = mass * shrink + jnp.sum(weights, axis=1, keepdims=True)
        mixed = mixed * shrink + jnp.dot(
            weights.astype(bf), keys[start : start + size, :latent], preferred_element_type=f32
        )
        return higher, mass, mixed

    for d in (0, 1, 3, 2):
        start = block(6, d)
        await_block(start, share // 2, d1_recv.at[d], y_dev)
        await_block(start + share // 2, share // 2, d2_recv.at[d], x_dev)
        send(start, block(7, d), share, s_recv.at[12 + d], sib_dev)
    for d in range(4):
        await_block(block(1, d), share, s_recv.at[d], sib_dev)
    top, mass, mixed = absorb_keys(0, 16 * share, top, mass, mixed)

    for group, at in ((4, 4), (5, 8), (7, 12)):
        for d in range(4):
            await_block(block(group, d), share, s_recv.at[at + d], sib_dev)
    top, mass, mixed = absorb_keys(16 * share, 16 * share, top, mass, mixed)

    mixed = (mixed / mass).astype(bf)
    value_load.wait()
    vdim = value.shape[2]
    live = out_ref.shape[0]
    alive = lax.broadcasted_iota(jnp.int32, (live, vdim), 0) % 8 < count_ref[0]
    for h in range(heads):
        up = jnp.dot(mixed[h * rows : (h + 1) * rows, :], value[h], preferred_element_type=f32)
        out_ref[:, h * vdim : (h + 1) * vdim] = jnp.where(alive, up[:live], 0.0).astype(bf)

    pair_a.wait_send()
    pair_b.wait_send()
    for copy in sends:
        copy.wait_send()


def local_fused(
    prefix_hidden,
    down_kv,
    latent_gain,
    step_hidden,
    query_nope,
    query_rope,
    key_absorb,
    value_up,
    cache,
    cache_len,
    counts,
):
    key_width = down_kv.shape[1]
    latent_width = latent_gain.shape[0]
    slots, steps, _ = step_hidden.shape
    heads, nope_width, _ = key_absorb.shape
    vdim = value_up.shape[2]
    logit_scale = (nope_width + key_width - latent_width) ** (-0.5)
    block_rows, model = prefix_hidden.shape
    share = block_rows // 2
    rows = 32

    def by_step(values):
        return values.transpose(1, 0, 2).reshape(steps * slots, -1)

    chunks = 7
    vmem = pl.BlockSpec(memory_space=pltpu.VMEM)
    smem = pl.BlockSpec(memory_space=pltpu.SMEM)
    hbm = pl.BlockSpec(memory_space=pltpu.HBM)
    dma = pltpu.SemaphoreType.DMA
    bf, f32 = jnp.bfloat16, jnp.float32
    operands = (
        cache_len,
        counts,
        prefix_hidden,
        by_step(step_hidden),
        down_kv.T,
        by_step(query_nope),
        by_step(query_rope),
        key_absorb,
        value_up,
        cache.transpose(0, 2, 1),
        latent_gain[None, :],
    )
    step_in, down_in, nope_in, rope_in = operands[3:7]
    out = pl.pallas_call(
        functools.partial(fused_kernel, chunks=chunks, logit_scale=logit_scale),
        out_shape=jax.ShapeDtypeStruct((steps * slots, heads * vdim), bf),
        in_specs=[smem, smem] + [hbm] * 9,
        out_specs=vmem,
        scratch_shapes=[
            pltpu.VMEM((block_rows + rows, model), bf),
            pltpu.VMEM(step_in.shape, bf),
            pltpu.VMEM(down_in.shape, bf),
            pltpu.VMEM(nope_in.shape, bf),
            pltpu.VMEM(rope_in.shape, bf),
            pltpu.VMEM(key_absorb.shape, bf),
            pltpu.VMEM(value_up.shape, bf),
            pltpu.VMEM(operands[9].shape, bf),
            pltpu.VMEM((1, latent_width), f32),
            pltpu.VMEM((128, key_width), bf),
            pltpu.VMEM((PREFIX, key_width), bf),
            pltpu.VMEM((heads * rows, key_width), bf),
            pltpu.VMEM((block_rows + rows, key_width), f32),
            pltpu.VMEM((share + rows, key_width), f32),
            dma((8 + chunks,)),
            dma((2,)),
            dma((2,)),
            dma((35,)),
            dma((4,)),
            dma((4,)),
            dma((4,)),
            dma((4,)),
            dma((4,)),
            dma((16,)),
        ],
        compiler_params=pltpu.CompilerParams(
            collective_id=0, has_side_effects=True, vmem_limit_bytes=62 * 1024 * 1024
        ),
    )(*operands)
    return out.reshape(steps, slots, heads * vdim).transpose(1, 0, 2)


def solution(mesh):
    in_specs = (
        P("dp", "tp"),
        P("tp", None),
        P(),
        P("dp", None, "tp"),
        P("dp", None, "tp"),
        P("dp", None, "tp"),
        P("tp", None, None),
        P("tp", None, None),
        P("dp", None, None),
        P("dp"),
        P("dp"),
    )
    out_specs = P("dp", None, "tp")
    fused = mesh.shape["dp"] == 16 and mesh.shape["tp"] == 2
    return jax.shard_map(local_fused if fused else local, mesh=mesh, in_specs=in_specs, out_specs=out_specs, check_vma=False)
```

```python
import functools

import jax
import jax.numpy as jnp
from jax import lax
from jax.experimental import pallas as pl
from jax.experimental.pallas import tpu as pltpu
from jax.sharding import PartitionSpec as P

PREFIX = 1024
MESH = pl.DeviceIdType.MESH
NEG = -1e30
LOG2E = 1.4426950408889634
LOG1E4 = 9.210340371976184


def apply_rotary_embedding(values, positions):
    half_width = values.shape[-1] // 2
    frequencies = 10000.0 ** (-jnp.arange(half_width, dtype=jnp.float32) / half_width)
    angles = positions[..., None] * frequencies
    cosine = jnp.cos(angles)
    sine_part = jnp.sin(angles)
    first_half = values[..., :half_width]
    second_half = values[..., half_width:]
    return jnp.concatenate(
        [
            first_half * cosine - second_half * sine_part,
            first_half * sine_part + second_half * cosine,
        ],
        axis=-1,
    )


def finish(raw_rows, gain, positions):
    latent_width = gain.shape[0]
    latent = raw_rows[..., :latent_width]
    factor = lax.rsqrt(jnp.mean(latent * latent, axis=-1, keepdims=True) + 1e-06)
    normed = latent * factor * gain
    return jnp.concatenate(
        [normed, apply_rotary_embedding(raw_rows[..., latent_width:], positions)], axis=-1
    ).astype(jnp.bfloat16)


def own_keys(
    query_entries,
    key_entries,
    lengths,
    row_max,
    row_mass,
    row_total,
    attention_head_count,
    logit_scale,
    latent_width,
):
    total_keys = key_entries.shape[1]
    context = total_keys - query_entries.shape[1] // attention_head_count
    scores = (
        jnp.einsum("aru,aeu->are", query_entries, key_entries, preferred_element_type=jnp.float32)
        * logit_scale
    )
    key_ids = jnp.arange(total_keys, dtype=jnp.int32)
    row_step = jnp.arange(query_entries.shape[1], dtype=jnp.int32) // attention_head_count
    new_ok = (key_ids[None, :] >= context) & (key_ids[None, :] - context <= row_step[:, None])
    is_valid = (key_ids[None, None, :] < lengths[:, None, None]) | new_ok[None]
    new_max = jnp.maximum(
        row_max, jnp.max(jnp.where(is_valid, scores, -1e30), axis=2, keepdims=True)
    )
    weights = jnp.where(is_valid, jnp.exp(scores - new_max), 0.0)
    shrink = jnp.exp(row_max - new_max)
    row_mass = row_mass * shrink + jnp.sum(weights, axis=2, keepdims=True)
    row_total = row_total * shrink + jnp.einsum(
        "dev,dva->dea",
        weights,
        key_entries[..., :latent_width].astype(jnp.float32),
        precision=lax.Precision.HIGHEST,
    )
    return (row_total / row_mass).astype(jnp.bfloat16)


def local(
    prefix_hidden,
    down_kv,
    latent_gain,
    step_hidden,
    query_nope,
    query_rope,
    key_absorb,
    value_up,
    cache,
    cache_len,
    counts,
):
    key_width = down_kv.shape[1]
    latent_width = latent_gain.shape[0]
    slot_count, step_count, _ = step_hidden.shape
    attention_head_count, nope_width, _ = key_absorb.shape
    rope_width = key_width - latent_width
    logit_scale = (nope_width + rope_width) ** (-0.5)
    partial_rows = jnp.dot(prefix_hidden, down_kv, preferred_element_type=jnp.float32)
    step_part = jnp.dot(
        step_hidden.reshape(slot_count * step_count, -1),
        down_kv,
        preferred_element_type=jnp.float32,
    )
    step_unprojected = lax.psum(step_part, "tp").reshape(slot_count, step_count, key_width)
    step_ids = jnp.arange(step_count, dtype=jnp.int32)
    new_pos = (PREFIX + cache_len[:, None] + step_ids[None, :]).astype(jnp.float32)
    new_keys = finish(step_unprojected, latent_gain, new_pos)
    nope_rows = query_nope.reshape(slot_count, step_count, attention_head_count, nope_width)
    query_latent = jnp.einsum(
        "stha,hal->sthl", nope_rows, key_absorb, preferred_element_type=jnp.float32
    ).astype(jnp.bfloat16)
    query_rot = apply_rotary_embedding(
        query_rope.reshape(slot_count, step_count, attention_head_count, rope_width).astype(
            jnp.float32
        ),
        new_pos[:, :, None],
    ).astype(jnp.bfloat16)
    queries = jnp.concatenate([query_latent, query_rot], axis=-1).reshape(
        slot_count * step_count * attention_head_count, key_width
    )
    total_rows = queries.shape[0]
    block_rows = partial_rows.shape[0]
    common_prompt_rows = lax.psum_scatter(partial_rows, "tp", scatter_dimension=0, tiled=True)
    share_count = common_prompt_rows.shape[0]
    first_row = lax.axis_index("dp") * block_rows + lax.axis_index("tp") * share_count
    positions = (first_row + jnp.arange(share_count, dtype=jnp.int32)).astype(jnp.float32)
    prefix_keys = finish(common_prompt_rows, latent_gain, positions)
    key_piece = lax.all_gather(prefix_keys, ("dp", "tp"), axis=0, tiled=True)
    row_max = jnp.full((total_rows, 1), -1e30, jnp.float32)
    scores = (
        jnp.einsum("qc,kc->qk", queries, key_piece, preferred_element_type=jnp.float32)
        * logit_scale
    )
    new_max = jnp.maximum(row_max, jnp.max(scores, axis=1, keepdims=True))
    weights = jnp.exp(scores - new_max)
    row_mass = jnp.sum(weights, axis=1, keepdims=True)
    row_total = jnp.dot(
        weights, key_piece[:, :latent_width].astype(jnp.float32), precision=lax.Precision.HIGHEST
    )
    row_max, row_mass, row_total = (new_max, row_mass, row_total)
    per_slot = step_count * attention_head_count
    query_slots = queries.reshape(slot_count, per_slot, key_width)
    row_max = row_max.reshape(slot_count, per_slot, 1)
    row_mass = row_mass.reshape(slot_count, per_slot, 1)
    row_total = row_total.reshape(slot_count, per_slot, latent_width)
    key_entries = jnp.concatenate([cache, new_keys], axis=1)
    live_count = counts[0]
    is_live = jnp.arange(slot_count, dtype=jnp.int32) < live_count
    latent_out = own_keys(
        query_slots,
        key_entries,
        cache_len,
        row_max,
        row_mass,
        row_total,
        attention_head_count,
        logit_scale,
        latent_width,
    )
    latent_out = latent_out.reshape(slot_count, step_count, attention_head_count, latent_width)
    projected = jnp.einsum(
        "sthl,hlv->sthv", latent_out, value_up, preferred_element_type=jnp.float32
    )
    projected = jnp.where(is_live[:, None, None, None], projected, 0.0)
    return projected.reshape(slot_count, step_count, -1).astype(jnp.bfloat16)


def rotate(x, cosine, signed_sine):
    lane = lax.broadcasted_iota(jnp.int32, x.shape, 1) % 64
    swapped = jnp.where(lane < 32, pltpu.roll(x, 96, 1), pltpu.roll(x, 32, 1))
    return x * cosine + swapped * signed_sine


def fused_kernel(
    len_ref,
    count_ref,
    prefix_hbm,
    step_hbm,
    down_hbm,
    nope_hbm,
    rope_hbm,
    absorb_hbm,
    value_hbm,
    cache_hbm,
    gain_hbm,
    out_ref,
    hidden,
    step,
    down,
    nope_rows,
    rope_rows,
    absorb,
    value,
    cache,
    gain,
    fresh,
    keys,
    queries,
    partial,
    arrived,
    load_sem,
    pair_send,
    pair_recv,
    send_sem,
    z_recv,
    x_recv,
    y_recv,
    d_recv,
    s_recv,
    *,
    chunks,
    logit_scale,
):
    dp = lax.axis_index("dp")
    tp = lax.axis_index("tp")
    z, y, x = dp // 4, (dp // 2) % 2, dp % 2
    latent = gain.shape[1]
    width = keys.shape[1]
    heads, nope, _ = absorb.shape
    slots, _, ctx = cache.shape
    share = 32
    rows = 32
    f32, bf = jnp.float32, jnp.bfloat16

    def place(zz, yy, xx):
        return zz * 4 + yy * 2 + xx

    x_dev = (place(z, y, 1 - x), tp)
    y_dev = (place(z, 1 - y, x), tp)
    xy_dev = (place(z, 1 - y, 1 - x), tp)
    sib_dev = (dp, 1 - tp)
    z_devs = {d: (place(lax.rem(z + d, 4), y, x), tp) for d in (1, 2, 3)}

    first_d = jnp.where(z == 0, 3, 1)
    second_d = jnp.where((z == 0) | (z == 3), 2, 3)
    third_d = jnp.where(z == 0, 1, jnp.where(z == 3, 3, 2))
    others = (first_d, second_d, third_d)
    barrier = pltpu.get_barrier_semaphore()
    for dev in (x_dev, y_dev, xy_dev, sib_dev, z_devs[1], z_devs[2], z_devs[3]):
        pl.semaphore_signal(barrier, inc=1, device_id=dev, device_id_type=MESH)

    prefix_rows, model = prefix_hbm.shape
    depth = model // chunks

    def load(src, dst, i):
        copy = pltpu.make_async_copy(src, dst, load_sem.at[i])
        copy.start()
        return copy

    step_load = load(step_hbm, step, 0)
    prefix_load = load(prefix_hbm, hidden.at[pl.ds(0, prefix_rows), :], 1)
    down_loads = []
    for i in range(chunks):
        span = pl.ds(i * depth, depth)
        down_loads.append(load(down_hbm.at[:, span], down.at[:, span], 8 + i))
    nope_load = load(nope_hbm, nope_rows, 2)
    rope_load = load(rope_hbm, rope_rows, 3)
    absorb_load = load(absorb_hbm, absorb, 4)
    gain_load = load(gain_hbm, gain, 5)
    cache_load = load(cache_hbm, cache, 6)
    value_load = load(value_hbm, value, 7)

    def padded(value_rows):
        wide = value_rows.astype(f32)
        return jnp.concatenate([wide, jnp.zeros((rows - wide.shape[0], wide.shape[1]), f32)], axis=0)

    sub = lax.broadcasted_iota(jnp.int32, (8, 128), 0)
    lane = lax.broadcasted_iota(jnp.int32, (8, 128), 1)
    lens = jnp.zeros((8, 128), jnp.int32)
    for s in range(slots):
        lens = jnp.where(sub == s, len_ref[s], lens)
    half = (width - latent) // 2
    frequency = jnp.exp((lane % half).astype(f32) * (-LOG1E4 / half))
    first = dp * prefix_rows + tp * share
    sign = jnp.where(lane % (2 * half) < half, -1.0, 1.0)
    cosines, sines = [], []
    for g in range((share + rows) // 8):
        if g < share // 8:
            position = first + g * 8 + sub
        else:
            position = PREFIX + lens + (g - share // 8)
        angle = position.astype(f32) * frequency
        cosines.append(jnp.cos(angle))
        sines.append(jnp.sin(angle) * sign)
    key_cos = jnp.concatenate(cosines[: share // 8], axis=0)
    key_sin = jnp.concatenate(sines[: share // 8], axis=0)
    step_cos = jnp.concatenate(cosines[share // 8 :], axis=0)
    step_sin = jnp.concatenate(sines[share // 8 :], axis=0)

    nt = (((1,), (1,)), ((), ()))
    step_load.wait()
    hidden[prefix_rows:, :] = padded(step[...]).astype(bf)
    prefix_load.wait()
    total = None
    for i in range(chunks):
        down_loads[i].wait()
        part = lax.dot_general(
            hidden[:, i * depth : (i + 1) * depth],
            down[:, i * depth : (i + 1) * depth],
            nt,
            preferred_element_type=f32,
        )
        total = part if total is None else total + part
    partial[...] = total

    pl.semaphore_wait(barrier, 7)
    theirs = pl.ds(pl.multiple_of((1 - tp) * share, share), share)
    mine = pl.ds(pl.multiple_of(tp * share, share), share)

    def remote(src, dst, ssem, rsem, dev):
        return pltpu.make_async_remote_copy(
            src_ref=src, dst_ref=dst, send_sem=ssem, recv_sem=rsem, device_id=dev, device_id_type=MESH
        )

    pair_a = remote(
        partial.at[theirs, :], arrived.at[pl.ds(0, share), :], pair_send.at[0], pair_recv.at[0], sib_dev
    )
    pair_b = remote(
        partial.at[pl.ds(prefix_rows, rows), :],
        arrived.at[pl.ds(share, rows), :],
        pair_send.at[1],
        pair_recv.at[1],
        sib_dev,
    )
    pair_a.start()
    pair_b.start()

    nope_load.wait()
    absorb_load.wait()
    nopes = padded(nope_rows[...]).astype(bf)
    for h in range(heads):
        ql = jnp.dot(nopes[:, h * nope : (h + 1) * nope], absorb[h], preferred_element_type=f32)
        queries[h * rows : (h + 1) * rows, :latent] = ql.astype(bf)
    rope_load.wait()
    ropes = padded(rope_rows[...])
    for p in range(heads // 2):
        turned = rotate(ropes[:, p * 128 : (p + 1) * 128], step_cos, step_sin).astype(bf)
        queries[2 * p * rows : (2 * p + 1) * rows, latent:] = turned[:, :64]
        queries[(2 * p + 1) * rows : (2 * p + 2) * rows, latent:] = turned[:, 64:]
    gain_load.wait()

    def finished(raw, cosine, signed_sine):
        low = raw[:, :latent]
        factor = lax.rsqrt(jnp.mean(low * low, axis=1, keepdims=True) + 1e-06)
        rope = raw[:, latent:]
        turned = rotate(jnp.concatenate([rope, rope], axis=1), cosine, signed_sine)
        return (low * factor * gain[...]).astype(bf), turned[:, : width - latent].astype(bf)

    pair_a.wait_recv()
    low, high = finished(partial[mine, :] + arrived[0:share, :], key_cos, key_sin)

    def block(group, d):
        at = (group * 4 + d) * share
        return at if isinstance(d, int) else pl.multiple_of(at, share)

    keys[0:share, :latent] = low
    keys[0:share, latent:] = high

    sends = []

    def send(source, target, size, rsem, dev):
        copy = remote(
            keys.at[pl.ds(source, size), :],
            keys.at[pl.ds(target, size), :],
            send_sem.at[len(sends)],
            rsem,
            dev,
        )
        copy.start()
        sends.append(copy)

    def await_block(start, size, rsem, dev):
        ref = keys.at[pl.ds(start, size), :]
        remote(ref, ref, send_sem.at[0], rsem, dev).wait_recv()

    def along(d):
        source = block(0, d)
        send(source, block(6, d), share, d_recv.at[d], xy_dev)
        send(source, block(2, d), share, x_recv.at[d], x_dev)
        send(source, block(3, d), share, y_recv.at[d], y_dev)
        send(source, block(1, d), share, s_recv.at[d], sib_dev)

    for d in (2, 1, 3):
        send(0, block(0, d), share, z_recv.at[d], z_devs[d])
    along(0)

    pair_b.wait_recv()
    low, high = finished(partial[prefix_rows:, :] + arrived[share:, :], step_cos, step_sin)
    fresh[0:rows, :latent] = low
    fresh[0:rows, latent:] = high
    fresh[rows:, :] = jnp.zeros((fresh.shape[0] - rows, width), bf)

    for d in others:
        await_block(block(0, d), share, z_recv.at[d], z_devs[1])
        along(d)

    cache_load.wait()
    q = queries[...]
    factor = logit_scale * LOG2E

    def own_scores(s):
        raw = jnp.dot(q, cache[s], preferred_element_type=f32).reshape(heads * rows // 8, 8, ctx)
        valid = (sub == s) & (lane < len_ref[s])
        return jnp.where(valid[None], raw, NEG).reshape(heads * rows, ctx)

    parts = [own_scores(s) for s in range(slots)]
    r32 = lax.broadcasted_iota(jnp.int32, (rows, 128), 0)
    c32 = lax.broadcasted_iota(jnp.int32, (rows, 128), 1)
    ok = (c32 % 8 == r32 % 8) & (c32 // 8 <= r32 // 8)
    raw = lax.dot_general(q, fresh[...], nt, preferred_element_type=f32).reshape(heads, rows, 128)
    parts.append(jnp.where(ok[None], raw, NEG).reshape(heads * rows, 128))

    def forward(d):
        source = block(2, d)
        await_block(source, share, x_recv.at[d], x_dev)
        send(source, block(4, d), share, s_recv.at[4 + d], sib_dev)
        source = block(3, d)
        await_block(source, share, y_recv.at[d], y_dev)
        send(source, block(5, d), share, s_recv.at[8 + d], sib_dev)

    for d in (0, *others):
        forward(d)

    top = functools.reduce(jnp.maximum, parts)
    top = jnp.max(top, axis=1, keepdims=True)
    mass, mixed = None, None
    weights = [jnp.exp2((part - top) * factor) for part in parts]
    mass = jnp.sum(functools.reduce(jnp.add, weights), axis=1, keepdims=True)
    mixed = jnp.dot(weights[slots].astype(bf), fresh[:, :latent], preferred_element_type=f32)
    for s in range(slots):
        mixed += lax.dot_general(
            weights[s].astype(bf), cache[s, :latent, :], nt, preferred_element_type=f32
        )

    def absorb_keys(start, size, top, mass, mixed):
        scores = lax.dot_general(q, keys[start : start + size, :], nt, preferred_element_type=f32)
        higher = jnp.maximum(top, jnp.max(scores, axis=1, keepdims=True))
        weights = jnp.exp2((scores - higher) * factor)
        shrink = jnp.exp2((top - higher) * factor)
        mass = mass * shrink + jnp.sum(weights, axis=1, keepdims=True)
        mixed = mixed * shrink + jnp.dot(
            weights.astype(bf), keys[start : start + size, :latent], preferred_element_type=f32
        )
        return higher, mass, mixed

    for d in (0, *others):
        start = block(6, d)
        await_block(start, share, d_recv.at[d], xy_dev)
        send(start, block(7, d), share, s_recv.at[12 + d], sib_dev)
    for d in range(4):
        await_block(block(1, d), share, s_recv.at[d], sib_dev)
    top, mass, mixed = absorb_keys(0, 16 * share, top, mass, mixed)

    for group, at in ((4, 4), (5, 8), (7, 12)):
        for d in range(4):
            await_block(block(group, d), share, s_recv.at[at + d], sib_dev)
    top, mass, mixed = absorb_keys(16 * share, 16 * share, top, mass, mixed)

    mixed = (mixed / mass).astype(bf)
    value_load.wait()
    vdim = value.shape[2]
    live = out_ref.shape[0]
    alive = lax.broadcasted_iota(jnp.int32, (live, vdim), 0) % 8 < count_ref[0]
    for h in range(heads):
        up = jnp.dot(mixed[h * rows : (h + 1) * rows, :], value[h], preferred_element_type=f32)
        out_ref[:, h * vdim : (h + 1) * vdim] = jnp.where(alive, up[:live], 0.0).astype(bf)

    pair_a.wait_send()
    pair_b.wait_send()
    for copy in sends:
        copy.wait_send()


def local_fused(
    prefix_hidden,
    down_kv,
    latent_gain,
    step_hidden,
    query_nope,
    query_rope,
    key_absorb,
    value_up,
    cache,
    cache_len,
    counts,
):
    key_width = down_kv.shape[1]
    latent_width = latent_gain.shape[0]
    slots, steps, _ = step_hidden.shape
    heads, nope_width, _ = key_absorb.shape
    vdim = value_up.shape[2]
    logit_scale = (nope_width + key_width - latent_width) ** (-0.5)
    block_rows, model = prefix_hidden.shape
    share = block_rows // 2
    rows = 32

    def by_step(values):
        return values.transpose(1, 0, 2).reshape(steps * slots, -1)

    chunks = 7
    vmem = pl.BlockSpec(memory_space=pltpu.VMEM)
    smem = pl.BlockSpec(memory_space=pltpu.SMEM)
    hbm = pl.BlockSpec(memory_space=pltpu.HBM)
    dma = pltpu.SemaphoreType.DMA
    bf, f32 = jnp.bfloat16, jnp.float32
    operands = (
        cache_len,
        counts,
        prefix_hidden,
        by_step(step_hidden),
        down_kv.T,
        by_step(query_nope),
        by_step(query_rope),
        key_absorb,
        value_up,
        cache.transpose(0, 2, 1),
        latent_gain[None, :],
    )
    step_in, down_in, nope_in, rope_in = operands[3:7]
    out = pl.pallas_call(
        functools.partial(fused_kernel, chunks=chunks, logit_scale=logit_scale),
        out_shape=jax.ShapeDtypeStruct((steps * slots, heads * vdim), bf),
        in_specs=[smem, smem] + [hbm] * 9,
        out_specs=vmem,
        scratch_shapes=[
            pltpu.VMEM((block_rows + rows, model), bf),
            pltpu.VMEM(step_in.shape, bf),
            pltpu.VMEM(down_in.shape, bf),
            pltpu.VMEM(nope_in.shape, bf),
            pltpu.VMEM(rope_in.shape, bf),
            pltpu.VMEM(key_absorb.shape, bf),
            pltpu.VMEM(value_up.shape, bf),
            pltpu.VMEM(operands[9].shape, bf),
            pltpu.VMEM((1, latent_width), f32),
            pltpu.VMEM((128, key_width), bf),
            pltpu.VMEM((PREFIX, key_width), bf),
            pltpu.VMEM((heads * rows, key_width), bf),
            pltpu.VMEM((block_rows + rows, key_width), f32),
            pltpu.VMEM((share + rows, key_width), f32),
            dma((8 + chunks,)),
            dma((2,)),
            dma((2,)),
            dma((31,)),
            dma((4,)),
            dma((4,)),
            dma((4,)),
            dma((4,)),
            dma((16,)),
        ],
        compiler_params=pltpu.CompilerParams(
            collective_id=0, has_side_effects=True, vmem_limit_bytes=62 * 1024 * 1024
        ),
    )(*operands)
    return out.reshape(steps, slots, heads * vdim).transpose(1, 0, 2)


def solution(mesh):
    in_specs = (
        P("dp", "tp"),
        P("tp", None),
        P(),
        P("dp", None, "tp"),
        P("dp", None, "tp"),
        P("dp", None, "tp"),
        P("tp", None, None),
        P("tp", None, None),
        P("dp", None, None),
        P("dp"),
        P("dp"),
    )
    out_specs = P("dp", None, "tp")
    fused = mesh.shape["dp"] == 16 and mesh.shape["tp"] == 2
    return jax.shard_map(local_fused if fused else local, mesh=mesh, in_specs=in_specs, out_specs=out_specs, check_vma=False)
```
